32 devices in a mesh: ctx: 16 (over z, x, core), tp: 2 (over y).
Axes of the slice: x: 2, y: 2, z: 4, core: 2. Of those that a mesh axis runs over, the one named last changes fastest.
Arguments:
- qkv_in: bfloat16 [2048, 3, 4096], P('ctx', None, 'tp'), may hold values from -6 to 6
- short_taps: float32 [3, 3, 4096], P(None, None, 'tp'), may hold values from -3.5 to 3.5
- long_filter: float32 [2048, 4096], P('ctx', 'tp'), may hold values from -1.7 to 1.7
- skip_gain: float32 [4096], P('tp'), may hold values from 0.2 to 1.5
- out_weight: bfloat16 [4096, 4096], P('tp', 'ctx'), may hold values from -0.125 to 0.125
Outputs:
- mixed_out: bfloat16 [2048, 4096], P('ctx', 'tp')
The draws below stay inside these ranges and needn't reach their ends.
All inputs are finite; a program needn't handle non-finite values.
Results may differ from the reference program's by a relative error of at most 0.0049.
Values may be sent and summed in bfloat16 or wider, within the bound.
No kernel may reach another device: no remote copies, remote signals or barrier semaphores. Data moves between devices by JAX's collectives and lax.ppermute only.
A program may use at most 128 MiB of HBM per device.

```python
import math
import jax
import jax.numpy as jnp
from jax import lax

D = 4096
SHORT_TAPS = 3
TOKENS = 2048


def draw_long_filter(key, part):
    key = jax.random.fold_in(key, 7)
    rate_key, tap_key = jax.random.split(key)
    positions = lax.iota(jnp.float32, TOKENS)[:, None]
    tap_noise = jnp.clip(jax.random.normal(tap_key, (TOKENS, D), jnp.float32), -6.0, 6.0)
    log_decay = jax.random.uniform(rate_key, (1, D), jnp.float32, math.log(30.0), math.log(2.0 * TOKENS))
    decay_len = jnp.exp(log_decay)
    return jnp.sqrt(2.0 / decay_len) * tap_noise * jnp.exp(-positions / decay_len)


def spiked(values, rng, source, target, parts, factor):
    owner, partner = [(jnp.arange(values.shape[axis_at]) // (values.shape[axis_at] // parts)).reshape([-1 if axis == axis_at else 1 for axis in range(values.ndim)]) for axis_at in (source, target)]
    chosen = jax.random.permutation(rng, parts)[partner]
    strong = (owner == chosen) | (owner == (partner + parts // 2) % parts)
    return jnp.where(strong, factor * values, values)


def level_of(rng, dims, cuts, smallest, largest):
    loudness, own = 1.0, jax.random.fold_in(rng, 6)
    for position, parts in cuts:
        draws = jnp.exp(jax.random.uniform(jax.random.fold_in(own, position), (parts,), jnp.float32, smallest / len(cuts), largest / len(cuts)))
        loudness = loudness * jnp.repeat(draws, dims[position] // parts).reshape([-1 if axis == position else 1 for axis in range(len(dims))])
    return loudness


def noise(rng, dims, scale, limit, cuts=(), held_as=jnp.bfloat16):
    array = jax.random.normal(rng, dims, jnp.float32) * scale
    if len(cuts) > 0:
        array = level_of(rng, dims, cuts, -0.22, 0.18) * array
    return jnp.clip(array, min=-limit, max=limit).astype(held_as)


def gaussian_with(key, extent, spread, bound, shards, heavy, dtype=jnp.bfloat16):
    values = spread * jax.random.normal(key, extent, jnp.float32)
    if shards:
        values = values * level_of(key, extent, shards, -0.22, 0.18)
    return jnp.clip(spiked(values, jax.random.fold_in(key, 3), *heavy), -bound, bound).astype(dtype)


def setup_inputs(seed: int = 0) -> dict:
    arg_keys = jax.random.split(jax.random.key(seed), 6)
    return {
        "qkv_in": noise(arg_keys[0], (TOKENS, 3, D), 1.0, 6.0, ((0, 16), (2, 2))),
        "short_taps": noise(arg_keys[1], (3, SHORT_TAPS, D), SHORT_TAPS ** -0.5, 3.5, ((2, 2),), jnp.float32),
        "long_filter": draw_long_filter(jax.random.fold_in(arg_keys[5], 71), 0),
        "skip_gain": jnp.clip(0.2 + 1.3 * jax.random.uniform(arg_keys[3], (D,), jnp.float32) ** level_of(arg_keys[3], (D,), ((0, 2),), -0.2, 0.2), 0.2, 1.5),
        "out_weight": gaussian_with(arg_keys[4], (D, D), D ** -0.5, 0.125, ((0, 2), (1, 16)), (0, 1, 16, 2.0)),
    }


def featurize(inputs, taps_one):
    tap_count = taps_one.shape[0]
    length = inputs.shape[0]
    padded = jnp.pad(inputs, ((tap_count - 1, 0), (0, 0)))
    result = jnp.zeros_like(inputs)
    for index_tap in range(tap_count):
        begin = tap_count - 1 - index_tap
        result = result + taps_one[index_tap][None, :] * padded[begin:begin + length]
    return result


def reference(qkv_in, short_taps, long_filter, skip_gain, out_weight):
    queries = featurize(qkv_in[:, 0, :].astype(jnp.float32), short_taps[0])
    keys_feat = featurize(qkv_in[:, 1, :].astype(jnp.float32), short_taps[1])
    values_feat = featurize(qkv_in[:, 2, :].astype(jnp.float32), short_taps[2])
    mixed_in = keys_feat * values_feat
    total_len = 2 * TOKENS
    spectrum = jnp.fft.rfft(mixed_in, n=total_len, axis=0) * jnp.fft.rfft(long_filter, n=total_len, axis=0)
    convolved = jnp.fft.irfft(spectrum, n=total_len, axis=0)[:TOKENS]
    gated_rows = (queries * (convolved + skip_gain[None, :] * mixed_in)).astype(jnp.bfloat16)
    return jnp.dot(gated_rows, out_weight, preferred_element_type=jnp.float32).astype(jnp.bfloat16)
```

```python
import functools
import itertools

import jax
import jax.numpy as jnp
import numpy as np
from jax import lax
from jax.experimental import pallas as pl
from jax.experimental.pallas import tpu as pltpu
from jax.sharding import PartitionSpec as P

BLOCK = 256
ROWS_AT_ONCE = 8
EDGE_ROWS = 16


def split_bf16(matrix):
    high = matrix.astype(jnp.bfloat16)
    low = (matrix - high.astype(np.float64)).astype(jnp.bfloat16)
    return high, low


@functools.cache
def transform_tables(block):
    freq = np.arange(block)[:, None] + 0.5
    radians = np.pi * freq * np.arange(block)[None, :] / block
    table = np.concatenate([np.cos(radians), -np.sin(radians)], axis=0)
    high, low = split_bf16(table)
    back_high, back_low = split_bf16(table.T / block)
    forward = np.concatenate([high, low], axis=1)
    backward = np.concatenate([back_high, back_low, back_high], axis=1)
    return forward, backward


def blocks_together(lanes, count):
    return 2 if lanes % 128 == 0 and count % 2 == 0 else 1


def forward_into(table_ref, read, count, spectra):
    together = blocks_together(read(0).shape[1], count)
    for first in range(0, count, together):
        columns = [read(first + i) for i in range(together)]
        wide = jnp.concatenate(columns, axis=1) if together > 1 else columns[0]
        spectrum = jnp.dot(
            table_ref[...],
            jnp.concatenate([wide, wide], axis=0),
            preferred_element_type=jnp.float32,
        )
        lanes = columns[0].shape[1]
        for i in range(together):
            spectra[first + i] = spectrum[:, i * lanes : (i + 1) * lanes]


def conv_kernel(
    table_ref,
    back_ref,
    arrived_ref,
    taps_ref,
    skip_ref,
    out_ref,
    spectra,
    filter_ref,
    products,
    padded,
    mixed,
    edges,
):
    block = table_ref.shape[1] // 2
    slabs, _, lanes = arrived_ref.shape
    tokens = mixed.shape[0]
    slab_rows = tokens // slabs
    count = tokens // block
    per_block = block // slab_rows

    def reader(kind):
        begin = kind * slab_rows

        def read(index):
            part = arrived_ref[
                index * per_block : (index + 1) * per_block, begin : begin + slab_rows
            ]
            return part.reshape(block, lanes)

        return read

    for index in range(count):
        mixed[index * block : (index + 1) * block] = reader(2)(index).astype(jnp.float32)
    complete_mixed(arrived_ref, taps_ref, mixed, edges)

    def read_mixed(index):
        return mixed[index * block : (index + 1) * block].astype(jnp.bfloat16)

    forward_into(table_ref, read_mixed, count, spectra)
    forward_into(table_ref, reader(0), count, filter_ref)

    parity = lax.broadcasted_iota(jnp.int32, (block, lanes), 0) % 2
    sign = (1 - 2 * parity).astype(jnp.float32)
    for index in range(count - 1, 0, -1):
        before_real = filter_ref[index - 1, :block]
        before_imag = filter_ref[index - 1, block:]
        filter_ref[index, :block] = filter_ref[index, :block] - sign * before_imag
        filter_ref[index, block:] = filter_ref[index, block:] + sign * before_real

    margin = padded.shape[0] - tokens
    padded[:margin] = jnp.zeros((margin, lanes), jnp.float32)
    for index in range(count):
        at = margin + index * block
        padded[at : at + block] = reader(1)(index).astype(jnp.float32)

    def rows_step(step, carry):
        at = pl.multiple_of(step * ROWS_AT_ONCE, ROWS_AT_ONCE)
        real_rows = pl.ds(at, ROWS_AT_ONCE)
        imag_rows = pl.ds(pl.multiple_of(block + at, ROWS_AT_ONCE), ROWS_AT_ONCE)
        signal_real = [spectra[i, real_rows] for i in range(count)]
        signal_imag = [spectra[i, imag_rows] for i in range(count)]
        filter_real = [filter_ref[i, real_rows] for i in range(count)]
        filter_imag = [filter_ref[i, imag_rows] for i in range(count)]
        for target in range(count):
            real = imag = None
            for source in range(target + 1):
                a, b = signal_real[source], signal_imag[source]
                c, d = filter_real[target - source], filter_imag[target - source]
                term_real = a * c - b * d
                term_imag = a * d + b * c
                real = term_real if real is None else real + term_real
                imag = term_imag if imag is None else imag + term_imag
            products[target, real_rows] = real
            products[target, imag_rows] = imag
        return carry

    def long_step(target, carry):
        def add(source, totals):
            a, b = spectra[source, :block], spectra[source, block:]
            c, d = filter_ref[target - source, :block], filter_ref[target - source, block:]
            return totals[0] + (a * c - b * d), totals[1] + (a * d + b * c)

        zero = jnp.zeros((block, lanes), jnp.float32)
        real, imag = lax.fori_loop(0, target + 1, add, (zero, zero))
        products[target, :block] = real
        products[target, block:] = imag
        return carry

    if count <= 8:
        lax.fori_loop(0, block // ROWS_AT_ONCE, rows_step, 0)
    else:
        lax.fori_loop(0, count, long_step, 0)

    together = blocks_together(lanes, count)
    for first in range(0, count, together):
        parts = [products[first + i] for i in range(together)]
        wide = jnp.concatenate(parts, axis=1) if together > 1 else parts[0]
        high = wide.astype(jnp.bfloat16)
        low = (wide - high.astype(jnp.float32)).astype(jnp.bfloat16)
        rows = jnp.dot(
            back_ref[...],
            jnp.concatenate([high, high, low], axis=0),
            preferred_element_type=jnp.float32,
        )
        for i in range(together):
            at = (first + i) * block
            convolved = rows[:, i * lanes : (i + 1) * lanes]
            begin = margin + at
            queries = taps_ref[0:1, :] * padded[begin : begin + block]
            for tap in range(1, taps_ref.shape[0] // 3):
                shifted = padded[begin - tap : begin - tap + block]
                queries = queries + taps_ref[tap : tap + 1, :] * shifted
            gated = queries * (convolved + skip_ref[...] * mixed[at : at + block])
            store_gated(out_ref, at, gated.astype(out_ref.dtype))


def complete_mixed(arrived_ref, taps_ref, mixed, edges):
    slabs = arrived_ref.shape[0]
    slab_rows = mixed.shape[0] // slabs
    taps = taps_ref.shape[0] // 3
    reach = taps - 1
    edges[:EDGE_ROWS] = jnp.zeros((EDGE_ROWS, edges.shape[1]), jnp.float32)
    for slab in range(slabs):
        at = (slab + 1) * EDGE_ROWS
        edges[at : at + EDGE_ROWS] = arrived_ref[slab, 3 * slab_rows :].astype(jnp.float32)

    def raw(kind, row):
        if row >= 0:
            return edges[pl.ds(EDGE_ROWS + kind * reach + row, slabs, stride=EDGE_ROWS), :]
        return edges[pl.ds((kind + 3) * reach + row, slabs, stride=EDGE_ROWS), :]

    for row in range(reach):
        product = None
        for kind in range(2):
            base = (kind + 1) * taps
            feature = taps_ref[base : base + 1, :] * raw(kind, row)
            for tap in range(1, taps):
                feature = feature + taps_ref[base + tap : base + tap + 1, :] * raw(kind, row - tap)
            product = feature if product is None else product * feature
        rounded = product.astype(jnp.bfloat16).astype(jnp.float32)
        mixed[pl.ds(row, slabs, stride=slab_rows), :] = rounded


def store_gated(out_ref, at, gated):
    copies, per_half, _, slab_rows, _ = out_ref.shape
    for begin in range(0, gated.shape[0], slab_rows):
        slab = (at + begin) // slab_rows
        for copy in range(copies):
            out_ref[copy, slab % per_half, slab // per_half] = gated[begin : begin + slab_rows]


def project_kernel(parts, own_ref, gated_ref, *refs):
    weight_refs, (near_ref, far_ref, rows) = iter(refs[:-3]), refs[-3:]
    sources, count, lanes = gated_ref.shape
    for source in range(sources):
        rows[:, source * lanes : (source + 1) * lanes] = gated_ref[source]
    swap = own_ref[0] == 1
    columns = near_ref.shape[1] // len(parts)
    for block, part_count in enumerate(parts):
        sums, begin = None, 0
        for weight_ref in itertools.islice(weight_refs, part_count):
            end = begin + weight_ref.shape[0]
            added = jnp.dot(rows[:, begin:end], weight_ref[...], preferred_element_type=jnp.float32)
            sums, begin = added if sums is None else sums + added, end
        first = sums[: count // 2].astype(near_ref.dtype)
        second = sums[count // 2 :].astype(near_ref.dtype)
        target = slice(block * columns, (block + 1) * columns)
        near_ref[:, target] = jnp.where(swap, second, first)
        far_ref[:, target] = jnp.where(swap, first, second)


def finish_kernel(first_offsets, place_ref, *refs):
    *pair_refs, out_ref = refs
    offset = 0
    for at, count in enumerate(first_offsets):
        near_ref, far_ref = pair_refs[2 * at : 2 * at + 2]
        columns = near_ref.shape[1] // count
        for block in range(count):
            source = slice(block * columns, (block + 1) * columns)
            total = near_ref[:, source].astype(jnp.float32) + far_ref[:, source].astype(jnp.float32)
            begin = (place_ref[0] ^ offset) * columns
            out_ref[:, pl.ds(pl.multiple_of(begin, columns), columns)] = total.astype(out_ref.dtype)
            offset += 1


def pack_kernel(qkv_ref, taps_ref, filter_ref, out_ref, padded, edges):
    targets, _, lanes = out_ref.shape
    rows = filter_ref.shape[0]
    reach = taps_ref.shape[1] - 1
    margin = padded.shape[0] - rows
    padded[:margin] = jnp.zeros((margin, padded.shape[1]), jnp.float32)
    edges[...] = jnp.zeros(edges.shape, jnp.float32)
    mixed_in = None
    for kind in (1, 2):
        padded[margin:] = qkv_ref[kind].astype(jnp.float32)
        feature = taps_ref[kind, 0:1] * padded[margin:]
        for tap in range(1, reach + 1):
            shifted = padded[margin - tap : margin - tap + rows]
            feature = feature + taps_ref[kind, tap : tap + 1] * shifted
        mixed_in = feature if mixed_in is None else mixed_in * feature
        edges[(kind - 1) * reach : kind * reach] = padded[margin : margin + reach]
        edges[(kind + 1) * reach : (kind + 2) * reach] = padded[margin + rows - reach :]
    for target in range(targets):
        at = slice(target * lanes, (target + 1) * lanes)
        out_ref[target, :rows] = filter_ref[:, at].astype(out_ref.dtype)
        out_ref[target, rows : 2 * rows] = qkv_ref[0, :, at]
        out_ref[target, 2 * rows : 3 * rows] = mixed_in[:, at].astype(out_ref.dtype)
        out_ref[target, 3 * rows :] = edges[:, at].astype(out_ref.dtype)


def pack(by_kind, short_taps, long_filter, peers):
    kinds, rows, channels = by_kind.shape
    reach = short_taps.shape[1] - 1
    lanes = channels // peers
    total = 3 * rows + EDGE_ROWS
    if lanes % 128:
        features = []
        for kind in (1, 2):
            extended = jnp.pad(by_kind[kind].astype(jnp.float32), ((reach, 0), (0, 0)))
            feature = short_taps[kind, 0] * extended[reach:]
            for tap in range(1, reach + 1):
                feature = feature + short_taps[kind, tap] * extended[reach - tap : reach - tap + rows]
            features.append(feature)
        mixed_in = (features[0] * features[1]).astype(jnp.bfloat16)
        first = by_kind[1:, :reach].reshape(2 * reach, channels)
        last = by_kind[1:, rows - reach :].reshape(2 * reach, channels)
        spare = jnp.zeros((EDGE_ROWS - 4 * reach, channels), jnp.bfloat16)
        parts = [long_filter.astype(jnp.bfloat16), by_kind[0], mixed_in, first, last, spare]
        return jnp.concatenate(parts).reshape(total, peers, lanes).transpose(1, 0, 2)
    steps = 2 if peers % 2 == 0 else 1
    width = channels // steps
    return pl.pallas_call(
        pack_kernel,
        out_shape=jax.ShapeDtypeStruct((peers, total, lanes), jnp.bfloat16),
        grid=(steps,),
        in_specs=[
            pl.BlockSpec((kinds, rows, width), lambda i: (0, 0, i)),
            pl.BlockSpec((kinds, reach + 1, width), lambda i: (0, 0, i)),
            pl.BlockSpec((rows, width), lambda i: (0, i)),
        ],
        out_specs=pl.BlockSpec((peers // steps, total, lanes), lambda i: (i, 0, 0)),
        scratch_shapes=[
            pltpu.VMEM((rows + 8, width), jnp.float32),
            pltpu.VMEM((EDGE_ROWS, width), jnp.float32),
        ],
        compiler_params=pltpu.CompilerParams(vmem_limit_bytes=60 * 2**20),
        cost_estimate=pl.CostEstimate(
            flops=16 * rows * channels, bytes_accessed=16 * rows * channels, transcendentals=0
        ),
        name="pack",
    )(by_kind, short_taps, long_filter)


def gated_conv(arrived, taps, skip, slab_rows, copies):
    slabs, _, lanes = arrived.shape
    tokens = slabs * slab_rows
    forward, backward = transform_tables(BLOCK)
    spectra = pltpu.VMEM((tokens // BLOCK, 2 * BLOCK, lanes), jnp.float32)
    return pl.pallas_call(
        conv_kernel,
        out_shape=jax.ShapeDtypeStruct(
            (copies, slabs // copies, copies, slab_rows, lanes), jnp.bfloat16
        ),
        scratch_shapes=[spectra] * 3
        + [
            pltpu.VMEM((tokens + 8, lanes), jnp.float32),
            pltpu.VMEM((tokens, lanes), jnp.float32),
            pltpu.VMEM(((slabs + 1) * EDGE_ROWS, lanes), jnp.float32),
        ],
        compiler_params=pltpu.CompilerParams(
            vmem_limit_bytes=(48 if tokens > 2048 else 20) * 2**20
        ),
        cost_estimate=pl.CostEstimate(
            flops=28 * BLOCK * tokens * lanes, bytes_accessed=20 * tokens * lanes, transcendentals=0
        ),
        name="gated_conv",
    )(jnp.asarray(forward), jnp.asarray(backward), arrived, taps, skip)


def project(own, gated, weights):
    sources, count, lanes = gated.shape
    depth, columns = sources * lanes, weights[0][0].shape[1]
    half = jax.ShapeDtypeStruct((count // 2, len(weights) * columns), jnp.bfloat16)
    whole = pl.BlockSpec(memory_space=pltpu.VMEM)
    flat = [part for parts in weights for part in parts]
    return pl.pallas_call(
        functools.partial(project_kernel, [len(parts) for parts in weights]),
        out_shape=(half, half),
        in_specs=[pl.BlockSpec(memory_space=pltpu.SMEM)] + [whole] * (1 + len(flat)),
        out_specs=(whole, whole),
        scratch_shapes=[pltpu.VMEM((count, depth), jnp.bfloat16)],
        compiler_params=pltpu.CompilerParams(vmem_limit_bytes=20 * 2**20),
        cost_estimate=pl.CostEstimate(
            flops=2 * count * depth * len(weights) * columns,
            bytes_accessed=2 * depth * len(weights) * columns + 4 * count * depth,
            transcendentals=0,
        ),
        name="project",
    )(own, gated, *flat)


def finish(place, pairs, blocks):
    rows = pairs[0][0].shape[0]
    columns = sum(near.shape[1] for near, _ in pairs)
    whole = pl.BlockSpec(memory_space=pltpu.VMEM)
    return pl.pallas_call(
        functools.partial(finish_kernel, blocks),
        out_shape=jax.ShapeDtypeStruct((rows, columns), jnp.bfloat16),
        in_specs=[pl.BlockSpec(memory_space=pltpu.SMEM)] + [whole] * (2 * len(pairs)),
        out_specs=whole,
        compiler_params=pltpu.CompilerParams(vmem_limit_bytes=20 * 2**20),
        cost_estimate=pl.CostEstimate(
            flops=rows * columns, bytes_accessed=6 * rows * columns, transcendentals=0
        ),
        name="finish",
    )(place, *[partial for pair in pairs for partial in pair])


def own_columns(array, lanes):
    return lax.dynamic_slice_in_dim(array, lax.axis_index("ctx") * lanes, lanes, axis=1)


def from_partner(value, offset):
    pairs = [(i, i ^ offset) for i in range(lax.axis_size("ctx"))]
    return lax.ppermute(value, "ctx", pairs)


def weights_on_the_way(out_weight):
    upper = out_weight[: out_weight.shape[0] // 2]
    return {0: [out_weight], 2: [from_partner(out_weight, 2)], 4: [from_partner(upper, 4)]}


def weights_passed_on(pieces, lower):
    return {**pieces, 4: pieces[4] + [from_partner(lower, 4)], 6: [from_partner(pieces[4][0], 2)]}


def weights_between_cores(pieces):
    pieces = {**pieces, 6: pieces[6] + [from_partner(pieces[4][1], 2)]}
    for at in (1, 3, 5, 7):
        pieces[at] = [from_partner(part, 1) for part in pieces[at ^ 1]]
    return [pieces[at] for at in range(8)]


def project_on_halves(gated, weights):
    half = lax.axis_size("ctx") // 2
    sources, halves, slab_rows, lanes = gated.shape
    rows = gated.reshape(sources, halves * slab_rows, lanes)
    own = lax.axis_index("tp").astype(jnp.int32)[None]
    place = (lax.axis_index("ctx") % half).astype(jnp.int32)[None]
    blocks = [len(weights) // 2] * 2
    arrived = []
    for part in (weights[: blocks[0]], weights[blocks[0] :]):
        partials = project(own, rows, part)
        arrived.append([to_their_place(partial, other) for other, partial in enumerate(partials)])
    return finish(place, arrived, blocks)


def to_their_place(partial, other):
    half = lax.axis_size("ctx") // 2
    pairs = []
    for side in range(2):
        for slab in range(half):
            for own in range(2):
                source = (side * half + slab) * 2 + own
                target = ((own ^ other) * half + slab) * 2 + side
                pairs.append((source, target))
    return lax.ppermute(partial, ("ctx", "tp"), pairs)


def project_whole(gated, out_weight):
    sources, _, slab_rows, lanes = gated.shape
    rows = gated.reshape(sources, slab_rows, lanes).transpose(1, 0, 2)
    partials = jnp.dot(
        rows.reshape(slab_rows, sources * lanes),
        lax.all_gather(out_weight, "ctx", axis=1, tiled=True),
        preferred_element_type=jnp.float32,
    )
    return lax.psum_scatter(partials, "tp", scatter_dimension=1, tiled=True).astype(jnp.bfloat16)


def body(qkv_in, short_taps, long_filter, skip_gain, out_weight):
    channel_count = qkv_in.shape[2]
    peers = lax.axis_size("ctx")
    lanes = channel_count // peers
    copies = 2 if lax.axis_size("tp") == 2 and peers == 16 else 1

    packed = pack(qkv_in.transpose(1, 0, 2), short_taps, long_filter, peers)
    arrived = lax.all_to_all(packed, "ctx", split_axis=0, concat_axis=0, tiled=True)
    if copies == 2:
        own_weight, _ = lax.optimization_barrier((out_weight, packed))
        pieces = weights_on_the_way(own_weight)
        lower = own_weight[own_weight.shape[0] // 2 :]
        (pieces, lower), _ = lax.optimization_barrier(((pieces, lower), arrived))
        pieces = weights_passed_on(pieces, lower)

    taps = own_columns(short_taps.reshape(-1, channel_count), lanes)
    skip = own_columns(skip_gain[None, :], lanes)
    gated = gated_conv(arrived, taps, skip, qkv_in.shape[0], copies)
    if copies == 2:
        gated, pieces = lax.optimization_barrier((gated, pieces))
        weights = weights_between_cores(pieces)
    by_target = gated.reshape(peers, copies, *gated.shape[3:])
    landed = lax.all_to_all(by_target, "ctx", split_axis=0, concat_axis=0, tiled=True)
    if copies == 2:
        return project_on_halves(landed, weights)
    return project_whole(landed, out_weight)


def solution(mesh):
    return jax.shard_map(
        body,
        mesh=mesh,
        in_specs=(
            P("ctx", None, "tp"),
            P(None, None, "tp"),
            P("ctx", "tp"),
            P("tp"),
            P("tp", "ctx"),
        ),
        out_specs=P("ctx", "tp"),
        check_vma=False,
    )
```

```python
import functools
import itertools

import jax
import jax.numpy as jnp
import numpy as np
from jax import lax
from jax.experimental import pallas as pl
from jax.experimental.pallas import tpu as pltpu
from jax.sharding import PartitionSpec as P

BLOCK = 256
ROWS_AT_ONCE = 8
EDGE_ROWS = 16


def split_bf16(matrix):
    high = matrix.astype(jnp.bfloat16)
    low = (matrix - high.astype(np.float64)).astype(jnp.bfloat16)
    return high, low


@functools.cache
def transform_tables(block):
    freq = np.arange(block)[:, None] + 0.5
    radians = np.pi * freq * np.arange(block)[None, :] / block
    table = np.concatenate([np.cos(radians), -np.sin(radians)], axis=0)
    high, low = split_bf16(table)
    back_high, back_low = split_bf16(table.T / block)
    forward = np.concatenate([high, low], axis=1)
    backward = np.concatenate([back_high, back_low, back_high], axis=1)
    return forward, backward


def blocks_together(lanes, count):
    return 2 if lanes % 128 == 0 and count % 2 == 0 else 1


def forward_into(table_ref, read, count, spectra):
    together = blocks_together(read(0).shape[1], count)
    for first in range(0, count, together):
        columns = [read(first + i) for i in range(together)]
        wide = jnp.concatenate(columns, axis=1) if together > 1 else columns[0]
        spectrum = jnp.dot(
            table_ref[...],
            jnp.concatenate([wide, wide], axis=0),
            preferred_element_type=jnp.float32,
        )
        lanes = columns[0].shape[1]
        for i in range(together):
            spectra[first + i] = spectrum[:, i * lanes : (i + 1) * lanes]


def conv_kernel(
    table_ref,
    back_ref,
    arrived_ref,
    taps_ref,
    skip_ref,
    out_ref,
    spectra,
    filter_ref,
    products,
    padded,
    mixed,
    edges,
):
    block = table_ref.shape[1] // 2
    slabs, _, lanes = arrived_ref.shape
    tokens = mixed.shape[0]
    slab_rows = tokens // slabs
    count = tokens // block
    per_block = block // slab_rows

    def reader(kind):
        begin = kind * slab_rows

        def read(index):
            part = arrived_ref[
                index * per_block : (index + 1) * per_block, begin : begin + slab_rows
            ]
            return part.reshape(block, lanes)

        return read

    for index in range(count):
        mixed[index * block : (index + 1) * block] = reader(2)(index).astype(jnp.float32)
    complete_mixed(arrived_ref, taps_ref, mixed, edges)

    def read_mixed(index):
        return mixed[index * block : (index + 1) * block].astype(jnp.bfloat16)

    forward_into(table_ref, read_mixed, count, spectra)
    forward_into(table_ref, reader(0), count, filter_ref)

    parity = lax.broadcasted_iota(jnp.int32, (block, lanes), 0) % 2
    sign = (1 - 2 * parity).astype(jnp.float32)
    for index in range(count - 1, 0, -1):
        before_real = filter_ref[index - 1, :block]
        before_imag = filter_ref[index - 1, block:]
        filter_ref[index, :block] = filter_ref[index, :block] - sign * before_imag
        filter_ref[index, block:] = filter_ref[index, block:] + sign * before_real

    margin = padded.shape[0] - tokens
    padded[:margin] = jnp.zeros((margin, lanes), jnp.float32)
    for index in range(count):
        at = margin + index * block
        padded[at : at + block] = reader(1)(index).astype(jnp.float32)

    def rows_step(step, carry):
        at = pl.multiple_of(step * ROWS_AT_ONCE, ROWS_AT_ONCE)
        real_rows = pl.ds(at, ROWS_AT_ONCE)
        imag_rows = pl.ds(pl.multiple_of(block + at, ROWS_AT_ONCE), ROWS_AT_ONCE)
        signal_real = [spectra[i, real_rows] for i in range(count)]
        signal_imag = [spectra[i, imag_rows] for i in range(count)]
        filter_real = [filter_ref[i, real_rows] for i in range(count)]
        filter_imag = [filter_ref[i, imag_rows] for i in range(count)]
        for target in range(count):
            real = imag = None
            for source in range(target + 1):
                a, b = signal_real[source], signal_imag[source]
                c, d = filter_real[target - source], filter_imag[target - source]
                term_real = a * c - b * d
                term_imag = a * d + b * c
                real = term_real if real is None else real + term_real
                imag = term_imag if imag is None else imag + term_imag
            products[target, real_rows] = real
            products[target, imag_rows] = imag
        return carry

    def long_step(target, carry):
        def add(source, totals):
            a, b = spectra[source, :block], spectra[source, block:]
            c, d = filter_ref[target - source, :block], filter_ref[target - source, block:]
            return totals[0] + (a * c - b * d), totals[1] + (a * d + b * c)

        zero = jnp.zeros((block, lanes), jnp.float32)
        real, imag = lax.fori_loop(0, target + 1, add, (zero, zero))
        products[target, :block] = real
        products[target, block:] = imag
        return carry

    if count <= 8:
        lax.fori_loop(0, block // ROWS_AT_ONCE, rows_step, 0)
    else:
        lax.fori_loop(0, count, long_step, 0)

    together = blocks_together(lanes, count)
    for first in range(0, count, together):
        parts = [products[first + i] for i in range(together)]
        wide = jnp.concatenate(parts, axis=1) if together > 1 else parts[0]
        high = wide.astype(jnp.bfloat16)
        low = (wide - high.astype(jnp.float32)).astype(jnp.bfloat16)
        rows = jnp.dot(
            back_ref[...],
            jnp.concatenate([high, high, low], axis=0),
            preferred_element_type=jnp.float32,
        )
        for i in range(together):
            at = (first + i) * block
            convolved = rows[:, i * lanes : (i + 1) * lanes]
            begin = margin + at
            queries = taps_ref[0:1, :] * padded[begin : begin + block]
            for tap in range(1, taps_ref.shape[0] // 3):
                shifted = padded[begin - tap : begin - tap + block]
                queries = queries + taps_ref[tap : tap + 1, :] * shifted
            gated = queries * (convolved + skip_ref[...] * mixed[at : at + block])
            store_gated(out_ref, at, gated.astype(out_ref.dtype))


def complete_mixed(arrived_ref, taps_ref, mixed, edges):
    slabs = arrived_ref.shape[0]
    slab_rows = mixed.shape[0] // slabs
    taps = taps_ref.shape[0] // 3
    reach = taps - 1
    edges[:EDGE_ROWS] = jnp.zeros((EDGE_ROWS, edges.shape[1]), jnp.float32)
    for slab in range(slabs):
        at = (slab + 1) * EDGE_ROWS
        edges[at : at + EDGE_ROWS] = arrived_ref[slab, 3 * slab_rows :].astype(jnp.float32)

    def raw(kind, row):
        if row >= 0:
            return edges[pl.ds(EDGE_ROWS + kind * reach + row, slabs, stride=EDGE_ROWS), :]
        return edges[pl.ds((kind + 3) * reach + row, slabs, stride=EDGE_ROWS), :]

    for row in range(reach):
        product = None
        for kind in range(2):
            base = (kind + 1) * taps
            feature = taps_ref[base : base + 1, :] * raw(kind, row)
            for tap in range(1, taps):
                feature = feature + taps_ref[base + tap : base + tap + 1, :] * raw(kind, row - tap)
            product = feature if product is None else product * feature
        rounded = product.astype(jnp.bfloat16).astype(jnp.float32)
        mixed[pl.ds(row, slabs, stride=slab_rows), :] = rounded


def store_gated(out_ref, at, gated):
    copies, per_half, _, slab_rows, _ = out_ref.shape
    for begin in range(0, gated.shape[0], slab_rows):
        slab = (at + begin) // slab_rows
        for copy in range(copies):
            out_ref[copy, slab % per_half, slab // per_half] = gated[begin : begin + slab_rows]


def project_kernel(parts, own_ref, gated_ref, *refs):
    weight_refs, (near_ref, far_ref, rows) = iter(refs[:-3]), refs[-3:]
    sources, count, lanes = gated_ref.shape
    for source in range(sources):
        rows[:, source * lanes : (source + 1) * lanes] = gated_ref[source]
    swap = own_ref[0] == 1
    columns = near_ref.shape[1] // len(parts)
    for block, part_count in enumerate(parts):
        sums, begin = None, 0
        for weight_ref in itertools.islice(weight_refs, part_count):
            end = begin + weight_ref.shape[0]
            added = jnp.dot(rows[:, begin:end], weight_ref[...], preferred_element_type=jnp.float32)
            sums, begin = added if sums is None else sums + added, end
        first = sums[: count // 2].astype(near_ref.dtype)
        second = sums[count // 2 :].astype(near_ref.dtype)
        target = slice(block * columns, (block + 1) * columns)
        near_ref[:, target] = jnp.where(swap, second, first)
        far_ref[:, target] = jnp.where(swap, first, second)


def finish_kernel(first_offsets, place_ref, *refs):
    *pair_refs, out_ref = refs
    offset = 0
    for at, count in enumerate(first_offsets):
        near_ref, far_ref = pair_refs[2 * at : 2 * at + 2]
        columns = near_ref.shape[1] // count
        for block in range(count):
            source = slice(block * columns, (block + 1) * columns)
            total = near_ref[:, source].astype(jnp.float32) + far_ref[:, source].astype(jnp.float32)
            begin = (place_ref[0] ^ offset) * columns
            out_ref[:, pl.ds(pl.multiple_of(begin, columns), columns)] = total.astype(out_ref.dtype)
            offset += 1


def pack_kernel(qkv_ref, taps_ref, filter_ref, out_ref, padded, edges):
    targets, _, lanes = out_ref.shape
    rows = filter_ref.shape[0]
    reach = taps_ref.shape[1] - 1
    margin = padded.shape[0] - rows
    padded[:margin] = jnp.zeros((margin, padded.shape[1]), jnp.float32)
    edges[...] = jnp.zeros(edges.shape, jnp.float32)
    mixed_in = None
    for kind in (1, 2):
        padded[margin:] = qkv_ref[kind].astype(jnp.float32)
        feature = taps_ref[kind, 0:1] * padded[margin:]
        for tap in range(1, reach + 1):
            shifted = padded[margin - tap : margin - tap + rows]
            feature = feature + taps_ref[kind, tap : tap + 1] * shifted
        mixed_in = feature if mixed_in is None else mixed_in * feature
        edges[(kind - 1) * reach : kind * reach] = padded[margin : margin + reach]
        edges[(kind + 1) * reach : (kind + 2) * reach] = padded[margin + rows - reach :]
    for target in range(targets):
        at = slice(target * lanes, (target + 1) * lanes)
        out_ref[target, :rows] = filter_ref[:, at].astype(out_ref.dtype)
        out_ref[target, rows : 2 * rows] = qkv_ref[0, :, at]
        out_ref[target, 2 * rows : 3 * rows] = mixed_in[:, at].astype(out_ref.dtype)
        out_ref[target, 3 * rows :] = edges[:, at].astype(out_ref.dtype)


def pack(by_kind, short_taps, long_filter, peers):
    kinds, rows, channels = by_kind.shape
    reach = short_taps.shape[1] - 1
    lanes = channels // peers
    total = 3 * rows + EDGE_ROWS
    if lanes % 128:
        features = []
        for kind in (1, 2):
            extended = jnp.pad(by_kind[kind].astype(jnp.float32), ((reach, 0), (0, 0)))
            feature = short_taps[kind, 0] * extended[reach:]
            for tap in range(1, reach + 1):
                feature = feature + short_taps[kind, tap] * extended[reach - tap : reach - tap + rows]
            features.append(feature)
        mixed_in = (features[0] * features[1]).astype(jnp.bfloat16)
        first = by_kind[1:, :reach].reshape(2 * reach, channels)
        last = by_kind[1:, rows - reach :].reshape(2 * reach, channels)
        spare = jnp.zeros((EDGE_ROWS - 4 * reach, channels), jnp.bfloat16)
        parts = [long_filter.astype(jnp.bfloat16), by_kind[0], mixed_in, first, last, spare]
        return jnp.concatenate(parts).reshape(total, peers, lanes).transpose(1, 0, 2)
    steps = 2 if peers % 2 == 0 else 1
    width = channels // steps
    return pl.pallas_call(
        pack_kernel,
        out_shape=jax.ShapeDtypeStruct((peers, total, lanes), jnp.bfloat16),
        grid=(steps,),
        in_specs=[
            pl.BlockSpec((kinds, rows, width), lambda i: (0, 0, i)),
            pl.BlockSpec((kinds, reach + 1, width), lambda i: (0, 0, i)),
            pl.BlockSpec((rows, width), lambda i: (0, i)),
        ],
        out_specs=pl.BlockSpec((peers // steps, total, lanes), lambda i: (i, 0, 0)),
        scratch_shapes=[
            pltpu.VMEM((rows + 8, width), jnp.float32),
            pltpu.VMEM((EDGE_ROWS, width), jnp.float32),
        ],
        compiler_params=pltpu.CompilerParams(vmem_limit_bytes=60 * 2**20),
        cost_estimate=pl.CostEstimate(
            flops=16 * rows * channels, bytes_accessed=16 * rows * channels, transcendentals=0
        ),
        name="pack",
    )(by_kind, short_taps, long_filter)


def gated_conv(arrived, taps, skip, slab_rows, copies):
    slabs, _, lanes = arrived.shape
    tokens = slabs * slab_rows
    forward, backward = transform_tables(BLOCK)
    spectra = pltpu.VMEM((tokens // BLOCK, 2 * BLOCK, lanes), jnp.float32)
    return pl.pallas_call(
        conv_kernel,
        out_shape=jax.ShapeDtypeStruct(
            (copies, slabs // copies, copies, slab_rows, lanes), jnp.bfloat16
        ),
        scratch_shapes=[spectra] * 3
        + [
            pltpu.VMEM((tokens + 8, lanes), jnp.float32),
            pltpu.VMEM((tokens, lanes), jnp.float32),
            pltpu.VMEM(((slabs + 1) * EDGE_ROWS, lanes), jnp.float32),
        ],
        compiler_params=pltpu.CompilerParams(
            vmem_limit_bytes=(48 if tokens > 2048 else 20) * 2**20
        ),
        cost_estimate=pl.CostEstimate(
            flops=28 * BLOCK * tokens * lanes, bytes_accessed=20 * tokens * lanes, transcendentals=0
        ),
        name="gated_conv",
    )(jnp.asarray(forward), jnp.asarray(backward), arrived, taps, skip)


def project(own, gated, weights):
    sources, count, lanes = gated.shape
    depth, columns = sources * lanes, weights[0][0].shape[1]
    half = jax.ShapeDtypeStruct((count // 2, len(weights) * columns), jnp.bfloat16)
    whole = pl.BlockSpec(memory_space=pltpu.VMEM)
    flat = [part for parts in weights for part in parts]
    return pl.pallas_call(
        functools.partial(project_kernel, [len(parts) for parts in weights]),
        out_shape=(half, half),
        in_specs=[pl.BlockSpec(memory_space=pltpu.SMEM)] + [whole] * (1 + len(flat)),
        out_specs=(whole, whole),
        scratch_shapes=[pltpu.VMEM((count, depth), jnp.bfloat16)],
        compiler_params=pltpu.CompilerParams(vmem_limit_bytes=20 * 2**20),
        cost_estimate=pl.CostEstimate(
            flops=2 * count * depth * len(weights) * columns,
            bytes_accessed=2 * depth * len(weights) * columns + 4 * count * depth,
            transcendentals=0,
        ),
        name="project",
    )(own, gated, *flat)


def finish(place, pairs, blocks):
    rows = pairs[0][0].shape[0]
    columns = sum(near.shape[1] for near, _ in pairs)
    whole = pl.BlockSpec(memory_space=pltpu.VMEM)
    return pl.pallas_call(
        functools.partial(finish_kernel, blocks),
        out_shape=jax.ShapeDtypeStruct((rows, columns), jnp.bfloat16),
        in_specs=[pl.BlockSpec(memory_space=pltpu.SMEM)] + [whole] * (2 * len(pairs)),
        out_specs=whole,
        compiler_params=pltpu.CompilerParams(vmem_limit_bytes=20 * 2**20),
        cost_estimate=pl.CostEstimate(
            flops=rows * columns, bytes_accessed=6 * rows * columns, transcendentals=0
        ),
        name="finish",
    )(place, *[partial for pair in pairs for partial in pair])


def own_columns(array, lanes):
    return lax.dynamic_slice_in_dim(array, lax.axis_index("ctx") * lanes, lanes, axis=1)


def from_partner(value, offset):
    pairs = [(i, i ^ offset) for i in range(lax.axis_size("ctx"))]
    return lax.ppermute(value, "ctx", pairs)


def weights_on_the_way(out_weight):
    upper = out_weight[: out_weight.shape[0] // 2]
    return {0: [out_weight], 2: [from_partner(out_weight, 2)], 4: [from_partner(upper, 4)]}


def weights_passed_on(pieces, lower):
    return {**pieces, 4: pieces[4] + [from_partner(lower, 4)], 6: [from_partner(pieces[4][0], 2)]}


def weights_between_cores(pieces):
    pieces = {**pieces, 6: pieces[6] + [from_partner(pieces[4][1], 2)]}
    for at in (1, 3, 5):
        pieces[at] = [from_partner(part, 1) for part in pieces[at ^ 1]]
    pieces[7] = [from_partner(pieces[6][0], 1)]
    return [pieces[at] for at in range(8)]


def project_on_halves(gated, weights):
    half = lax.axis_size("ctx") // 2
    sources, halves, slab_rows, lanes = gated.shape
    rows = gated.reshape(sources, halves * slab_rows, lanes)
    own = lax.axis_index("tp").astype(jnp.int32)[None]
    place = (lax.axis_index("ctx") % half).astype(jnp.int32)[None]
    split = len(weights) // 2
    first = project(own, rows, weights[:split])
    last_part, _ = lax.optimization_barrier((weights[6][-1], first[0]))
    weights[7] = weights[7] + [from_partner(last_part, 1)]
    second = project(own, rows, weights[split:])
    arrived = [
        [to_their_place(partial, other) for other, partial in enumerate(partials)]
        for partials in (first, second)
    ]
    return finish(place, arrived, [split, len(weights) - split])


def to_their_place(partial, other):
    half = lax.axis_size("ctx") // 2
    pairs = []
    for side in range(2):
        for slab in range(half):
            for own in range(2):
                source = (side * half + slab) * 2 + own
                target = ((own ^ other) * half + slab) * 2 + side
                pairs.append((source, target))
    return lax.ppermute(partial, ("ctx", "tp"), pairs)


def project_whole(gated, out_weight):
    sources, _, slab_rows, lanes = gated.shape
    rows = gated.reshape(sources, slab_rows, lanes).transpose(1, 0, 2)
    partials = jnp.dot(
        rows.reshape(slab_rows, sources * lanes),
        lax.all_gather(out_weight, "ctx", axis=1, tiled=True),
        preferred_element_type=jnp.float32,
    )
    return lax.psum_scatter(partials, "tp", scatter_dimension=1, tiled=True).astype(jnp.bfloat16)


def body(qkv_in, short_taps, long_filter, skip_gain, out_weight):
    channel_count = qkv_in.shape[2]
    peers = lax.axis_size("ctx")
    lanes = channel_count // peers
    copies = 2 if lax.axis_size("tp") == 2 and peers == 16 else 1

    packed = pack(qkv_in.transpose(1, 0, 2), short_taps, long_filter, peers)
    arrived = lax.all_to_all(packed, "ctx", split_axis=0, concat_axis=0, tiled=True)
    if copies == 2:
        own_weight, _ = lax.optimization_barrier((out_weight, packed))
        pieces = weights_on_the_way(own_weight)
        lower = own_weight[own_weight.shape[0] // 2 :]
        (pieces, lower), _ = lax.optimization_barrier(((pieces, lower), arrived))
        pieces = weights_passed_on(pieces, lower)

    taps = own_columns(short_taps.reshape(-1, channel_count), lanes)
    skip = own_columns(skip_gain[None, :], lanes)
    gated = gated_conv(arrived, taps, skip, qkv_in.shape[0], copies)
    if copies == 2:
        gated, pieces = lax.optimization_barrier((gated, pieces))
        weights = weights_between_cores(pieces)
    by_target = gated.reshape(peers, copies, *gated.shape[3:])
    landed = lax.all_to_all(by_target, "ctx", split_axis=0, concat_axis=0, tiled=True)
    if copies == 2:
        return project_on_halves(landed, weights)
    return project_whole(landed, out_weight)


def solution(mesh):
    return jax.shard_map(
        body,
        mesh=mesh,
        in_specs=(
            P("ctx", None, "tp"),
            P(None, None, "tp"),
            P("ctx", "tp"),
            P("tp"),
            P("tp", "ctx"),
        ),
        out_specs=P("ctx", "tp"),
        check_vma=False,
    )
```

```python
import functools
import itertools

import jax
import jax.numpy as jnp
import numpy as np
from jax import lax
from jax.experimental import pallas as pl
from jax.experimental.pallas import tpu as pltpu
from jax.sharding import PartitionSpec as P

BLOCK = 256
ROWS_AT_ONCE = 8
EDGE_ROWS = 16


def split_bf16(matrix):
    high = matrix.astype(jnp.bfloat16)
    low = (matrix - high.astype(np.float64)).astype(jnp.bfloat16)
    return high, low


@functools.cache
def transform_tables(block):
    freq = np.arange(block)[:, None] + 0.5
    radians = np.pi * freq * np.arange(block)[None, :] / block
    table = np.concatenate([np.cos(radians), -np.sin(radians)], axis=0)
    high, low = split_bf16(table)
    back_high, back_low = split_bf16(table.T / block)
    forward = np.concatenate([high, low], axis=1)
    backward = np.concatenate([back_high, back_low, back_high], axis=1)
    return forward, backward


def blocks_together(lanes, count):
    return 2 if lanes % 128 == 0 and count % 2 == 0 else 1


def forward_into(table_ref, read, count, spectra):
    together = blocks_together(read(0).shape[1], count)
    for first in range(0, count, together):
        columns = [read(first + i) for i in range(together)]
        wide = jnp.concatenate(columns, axis=1) if together > 1 else columns[0]
        spectrum = jnp.dot(
            table_ref[...],
            jnp.concatenate([wide, wide], axis=0),
            preferred_element_type=jnp.float32,
        )
        lanes = columns[0].shape[1]
        for i in range(together):
            spectra[first + i] = spectrum[:, i * lanes : (i + 1) * lanes]


def conv_kernel(
    table_ref,
    back_ref,
    arrived_ref,
    taps_ref,
    skip_ref,
    out_ref,
    spectra,
    filter_ref,
    products,
    padded,
    mixed,
    edges,
):
    block = table_ref.shape[1] // 2
    slabs, _, lanes = arrived_ref.shape
    tokens = mixed.shape[0]
    slab_rows = tokens // slabs
    count = tokens // block
    per_block = block // slab_rows

    def reader(kind):
        begin = kind * slab_rows

        def read(index):
            part = arrived_ref[
                index * per_block : (index + 1) * per_block, begin : begin + slab_rows
            ]
            return part.reshape(block, lanes)

        return read

    for index in range(count):
        mixed[index * block : (index + 1) * block] = reader(2)(index).astype(jnp.float32)
    complete_mixed(arrived_ref, taps_ref, mixed, edges)

    def read_mixed(index):
        return mixed[index * block : (index + 1) * block].astype(jnp.bfloat16)

    forward_into(table_ref, read_mixed, count, spectra)
    forward_into(table_ref, reader(0), count, filter_ref)

    parity = lax.broadcasted_iota(jnp.int32, (block, lanes), 0) % 2
    sign = (1 - 2 * parity).astype(jnp.float32)
    for index in range(count - 1, 0, -1):
        before_real = filter_ref[index - 1, :block]
        before_imag = filter_ref[index - 1, block:]
        filter_ref[index, :block] = filter_ref[index, :block] - sign * before_imag
        filter_ref[index, block:] = filter_ref[index, block:] + sign * before_real

    margin = padded.shape[0] - tokens
    padded[:margin] = jnp.zeros((margin, lanes), jnp.float32)
    for index in range(count):
        at = margin + index * block
        padded[at : at + block] = reader(1)(index).astype(jnp.float32)

    def rows_step(step, carry):
        at = pl.multiple_of(step * ROWS_AT_ONCE, ROWS_AT_ONCE)
        real_rows = pl.ds(at, ROWS_AT_ONCE)
        imag_rows = pl.ds(pl.multiple_of(block + at, ROWS_AT_ONCE), ROWS_AT_ONCE)
        signal_real = [spectra[i, real_rows] for i in range(count)]
        signal_imag = [spectra[i, imag_rows] for i in range(count)]
        filter_real = [filter_ref[i, real_rows] for i in range(count)]
        filter_imag = [filter_ref[i, imag_rows] for i in range(count)]
        for target in range(count):
            real = imag = None
            for source in range(target + 1):
                a, b = signal_real[source], signal_imag[source]
                c, d = filter_real[target - source], filter_imag[target - source]
                term_real = a * c - b * d
                term_imag = a * d + b * c
                real = term_real if real is None else real + term_real
                imag = term_imag if imag is None else imag + term_imag
            products[target, real_rows] = real
            products[target, imag_rows] = imag
        return carry

    def long_step(target, carry):
        def add(source, totals):
            a, b = spectra[source, :block], spectra[source, block:]
            c, d = filter_ref[target - source, :block], filter_ref[target - source, block:]
            return totals[0] + (a * c - b * d), totals[1] + (a * d + b * c)

        zero = jnp.zeros((block, lanes), jnp.float32)
        real, imag = lax.fori_loop(0, target + 1, add, (zero, zero))
        products[target, :block] = real
        products[target, block:] = imag
        return carry

    if count <= 8:
        lax.fori_loop(0, block // ROWS_AT_ONCE, rows_step, 0)
    else:
        lax.fori_loop(0, count, long_step, 0)

    together = blocks_together(lanes, count)
    for first in range(0, count, together):
        parts = [products[first + i] for i in range(together)]
        wide = jnp.concatenate(parts, axis=1) if together > 1 else parts[0]
        high = wide.astype(jnp.bfloat16)
        low = (wide - high.astype(jnp.float32)).astype(jnp.bfloat16)
        rows = jnp.dot(
            back_ref[...],
            jnp.concatenate([high, high, low], axis=0),
            preferred_element_type=jnp.float32,
        )
        for i in range(together):
            at = (first + i) * block
            convolved = rows[:, i * lanes : (i + 1) * lanes]
            begin = margin + at
            queries = taps_ref[0:1, :] * padded[begin : begin + block]
            for tap in range(1, taps_ref.shape[0] // 3):
                shifted = padded[begin - tap : begin - tap + block]
                queries = queries + taps_ref[tap : tap + 1, :] * shifted
            gated = queries * (convolved + skip_ref[...] * mixed[at : at + block])
            store_gated(out_ref, at, gated.astype(out_ref.dtype))


def complete_mixed(arrived_ref, taps_ref, mixed, edges):
    slabs = arrived_ref.shape[0]
    slab_rows = mixed.shape[0] // slabs
    taps = taps_ref.shape[0] // 3
    reach = taps - 1
    edges[:EDGE_ROWS] = jnp.zeros((EDGE_ROWS, edges.shape[1]), jnp.float32)
    for slab in range(slabs):
        at = (slab + 1) * EDGE_ROWS
        edges[at : at + EDGE_ROWS] = arrived_ref[slab, 3 * slab_rows :].astype(jnp.float32)

    def raw(kind, row):
        if row >= 0:
            return edges[pl.ds(EDGE_ROWS + kind * reach + row, slabs, stride=EDGE_ROWS), :]
        return edges[pl.ds((kind + 3) * reach + row, slabs, stride=EDGE_ROWS), :]

    for row in range(reach):
        product = None
        for kind in range(2):
            base = (kind + 1) * taps
            feature = taps_ref[base : base + 1, :] * raw(kind, row)
            for tap in range(1, taps):
                feature = feature + taps_ref[base + tap : base + tap + 1, :] * raw(kind, row - tap)
            product = feature if product is None else product * feature
        rounded = product.astype(jnp.bfloat16).astype(jnp.float32)
        mixed[pl.ds(row, slabs, stride=slab_rows), :] = rounded


def store_gated(out_ref, at, gated):
    copies, per_half, _, slab_rows, _ = out_ref.shape
    for begin in range(0, gated.shape[0], slab_rows):
        slab = (at + begin) // slab_rows
        for copy in range(copies):
            out_ref[copy, slab % per_half, slab // per_half] = gated[begin : begin + slab_rows]


def project_kernel(parts, own_ref, gated_ref, *refs):
    weight_refs, (near_ref, far_ref, rows) = iter(refs[:-3]), refs[-3:]
    sources, count, lanes = gated_ref.shape
    for source in range(sources):
        rows[:, source * lanes : (source + 1) * lanes] = gated_ref[source]
    swap = own_ref[0] == 1
    columns = near_ref.shape[1] // len(parts)
    for block, part_count in enumerate(parts):
        sums, begin = None, 0
        for weight_ref in itertools.islice(weight_refs, part_count):
            end = begin + weight_ref.shape[0]
            added = jnp.dot(rows[:, begin:end], weight_ref[...], preferred_element_type=jnp.float32)
            sums, begin = added if sums is None else sums + added, end
        first = sums[: count // 2].astype(near_ref.dtype)
        second = sums[count // 2 :].astype(near_ref.dtype)
        target = slice(block * columns, (block + 1) * columns)
        near_ref[:, target] = jnp.where(swap, second, first)
        far_ref[:, target] = jnp.where(swap, first, second)


def finish_kernel(first_offsets, place_ref, *refs):
    *pair_refs, out_ref = refs
    offset = 0
    for at, count in enumerate(first_offsets):
        near_ref, far_ref = pair_refs[2 * at : 2 * at + 2]
        columns = near_ref.shape[1] // count
        for block in range(count):
            source = slice(block * columns, (block + 1) * columns)
            total = near_ref[:, source].astype(jnp.float32) + far_ref[:, source].astype(jnp.float32)
            begin = (place_ref[0] ^ offset) * columns
            out_ref[:, pl.ds(pl.multiple_of(begin, columns), columns)] = total.astype(out_ref.dtype)
            offset += 1


def pack_kernel(qkv_ref, taps_ref, filter_ref, out_ref, padded, edges):
    targets, _, lanes = out_ref.shape
    rows = filter_ref.shape[0]
    reach = taps_ref.shape[1] - 1
    margin = padded.shape[0] - rows
    padded[:margin] = jnp.zeros((margin, padded.shape[1]), jnp.float32)
    edges[...] = jnp.zeros(edges.shape, jnp.float32)
    mixed_in = None
    for kind in (1, 2):
        padded[margin:] = qkv_ref[kind].astype(jnp.float32)
        feature = taps_ref[kind, 0:1] * padded[margin:]
        for tap in range(1, reach + 1):
            shifted = padded[margin - tap : margin - tap + rows]
            feature = feature + taps_ref[kind, tap : tap + 1] * shifted
        mixed_in = feature if mixed_in is None else mixed_in * feature
        edges[(kind - 1) * reach : kind * reach] = padded[margin : margin + reach]
        edges[(kind + 1) * reach : (kind + 2) * reach] = padded[margin + rows - reach :]
    for target in range(targets):
        at = slice(target * lanes, (target + 1) * lanes)
        out_ref[target, :rows] = filter_ref[:, at].astype(out_ref.dtype)
        out_ref[target, rows : 2 * rows] = qkv_ref[0, :, at]
        out_ref[target, 2 * rows : 3 * rows] = mixed_in[:, at].astype(out_ref.dtype)
        out_ref[target, 3 * rows :] = edges[:, at].astype(out_ref.dtype)


def pack(by_kind, short_taps, long_filter, peers):
    kinds, rows, channels = by_kind.shape
    reach = short_taps.shape[1] - 1
    lanes = channels // peers
    total = 3 * rows + EDGE_ROWS
    if lanes % 128:
        features = []
        for kind in (1, 2):
            extended = jnp.pad(by_kind[kind].astype(jnp.float32), ((reach, 0), (0, 0)))
            feature = short_taps[kind, 0] * extended[reach:]
            for tap in range(1, reach + 1):
                feature = feature + short_taps[kind, tap] * extended[reach - tap : reach - tap + rows]
            features.append(feature)
        mixed_in = (features[0] * features[1]).astype(jnp.bfloat16)
        first = by_kind[1:, :reach].reshape(2 * reach, channels)
        last = by_kind[1:, rows - reach :].reshape(2 * reach, channels)
        spare = jnp.zeros((EDGE_ROWS - 4 * reach, channels), jnp.bfloat16)
        parts = [long_filter.astype(jnp.bfloat16), by_kind[0], mixed_in, first, last, spare]
        return jnp.concatenate(parts).reshape(total, peers, lanes).transpose(1, 0, 2)
    steps = 2 if peers % 2 == 0 else 1
    width = channels // steps
    return pl.pallas_call(
        pack_kernel,
        out_shape=jax.ShapeDtypeStruct((peers, total, lanes), jnp.bfloat16),
        grid=(steps,),
        in_specs=[
            pl.BlockSpec((kinds, rows, width), lambda i: (0, 0, i)),
            pl.BlockSpec((kinds, reach + 1, width), lambda i: (0, 0, i)),
            pl.BlockSpec((rows, width), lambda i: (0, i)),
        ],
        out_specs=pl.BlockSpec((peers // steps, total, lanes), lambda i: (i, 0, 0)),
        scratch_shapes=[
            pltpu.VMEM((rows + 8, width), jnp.float32),
            pltpu.VMEM((EDGE_ROWS, width), jnp.float32),
        ],
        compiler_params=pltpu.CompilerParams(vmem_limit_bytes=60 * 2**20),
        cost_estimate=pl.CostEstimate(
            flops=16 * rows * channels, bytes_accessed=16 * rows * channels, transcendentals=0
        ),
        name="pack",
    )(by_kind, short_taps, long_filter)


def gated_conv(arrived, taps, skip, slab_rows, copies):
    slabs, _, lanes = arrived.shape
    tokens = slabs * slab_rows
    forward, backward = transform_tables(BLOCK)
    spectra = pltpu.VMEM((tokens // BLOCK, 2 * BLOCK, lanes), jnp.float32)
    return pl.pallas_call(
        conv_kernel,
        out_shape=jax.ShapeDtypeStruct(
            (copies, slabs // copies, copies, slab_rows, lanes), jnp.bfloat16
        ),
        scratch_shapes=[spectra] * 3
        + [
            pltpu.VMEM((tokens + 8, lanes), jnp.float32),
            pltpu.VMEM((tokens, lanes), jnp.float32),
            pltpu.VMEM(((slabs + 1) * EDGE_ROWS, lanes), jnp.float32),
        ],
        compiler_params=pltpu.CompilerParams(
            vmem_limit_bytes=(48 if tokens > 2048 else 20) * 2**20
        ),
        cost_estimate=pl.CostEstimate(
            flops=28 * BLOCK * tokens * lanes, bytes_accessed=20 * tokens * lanes, transcendentals=0
        ),
        name="gated_conv",
    )(jnp.asarray(forward), jnp.asarray(backward), arrived, taps, skip)


def project(own, gated, weights):
    sources, count, lanes = gated.shape
    depth, columns = sources * lanes, weights[0][0].shape[1]
    half = jax.ShapeDtypeStruct((count // 2, len(weights) * columns), jnp.bfloat16)
    whole = pl.BlockSpec(memory_space=pltpu.VMEM)
    flat = [part for parts in weights for part in parts]
    return pl.pallas_call(
        functools.partial(project_kernel, [len(parts) for parts in weights]),
        out_shape=(half, half),
        in_specs=[pl.BlockSpec(memory_space=pltpu.SMEM)] + [whole] * (1 + len(flat)),
        out_specs=(whole, whole),
        scratch_shapes=[pltpu.VMEM((count, depth), jnp.bfloat16)],
        compiler_params=pltpu.CompilerParams(vmem_limit_bytes=20 * 2**20),
        cost_estimate=pl.CostEstimate(
            flops=2 * count * depth * len(weights) * columns,
            bytes_accessed=2 * depth * len(weights) * columns + 4 * count * depth,
            transcendentals=0,
        ),
        name="project",
    )(own, gated, *flat)


def finish(place, pairs, blocks):
    rows = pairs[0][0].shape[0]
    columns = sum(near.shape[1] for near, _ in pairs)
    whole = pl.BlockSpec(memory_space=pltpu.VMEM)
    return pl.pallas_call(
        functools.partial(finish_kernel, blocks),
        out_shape=jax.ShapeDtypeStruct((rows, columns), jnp.bfloat16),
        in_specs=[pl.BlockSpec(memory_space=pltpu.SMEM)] + [whole] * (2 * len(pairs)),
        out_specs=whole,
        compiler_params=pltpu.CompilerParams(vmem_limit_bytes=20 * 2**20),
        cost_estimate=pl.CostEstimate(
            flops=rows * columns, bytes_accessed=6 * rows * columns, transcendentals=0
        ),
        name="finish",
    )(place, *[partial for pair in pairs for partial in pair])


def own_columns(array, lanes):
    return lax.dynamic_slice_in_dim(array, lax.axis_index("ctx") * lanes, lanes, axis=1)


def from_partner(value, offset):
    pairs = [(i, i ^ offset) for i in range(lax.axis_size("ctx"))]
    return lax.ppermute(value, "ctx", pairs)


def after(values, *others):
    return lax.optimization_barrier((values, others))[0]


def weights_from_chips(out_weight, packed, arrived):
    cut = out_weight.shape[0] // 16 * 7
    own = after(out_weight, packed)
    x_piece = from_partner(own, 2)
    z_first, rest = after((from_partner(own[:cut], 4), own[cut:]), arrived)
    return {
        0: [out_weight],
        2: [x_piece],
        4: [z_first, from_partner(rest, 4)],
        6: [from_partner(z_first, 2)],
    }


def weights_between_cores(pieces):
    pieces = {**pieces, 6: pieces[6] + [from_partner(pieces[4][1], 2)]}
    for at in (1, 3, 5):
        pieces[at] = [from_partner(part, 1) for part in pieces[at ^ 1]]
    pieces[7] = [from_partner(pieces[6][0], 1)]
    return [pieces[at] for at in range(8)]


def project_on_halves(gated, weights):
    half = lax.axis_size("ctx") // 2
    sources, halves, slab_rows, lanes = gated.shape
    rows = gated.reshape(sources, halves * slab_rows, lanes)
    own = lax.axis_index("tp").astype(jnp.int32)[None]
    place = (lax.axis_index("ctx") % half).astype(jnp.int32)[None]
    split = len(weights) // 2
    first = project(own, rows, weights[:split])
    last_part, _ = lax.optimization_barrier((weights[6][-1], first[0]))
    weights[7] = weights[7] + [from_partner(last_part, 1)]
    second = project(own, rows, weights[split:])
    arrived = [
        [to_their_place(partial, other) for other, partial in enumerate(partials)]
        for partials in (first, second)
    ]
    return finish(place, arrived, [split, len(weights) - split])


def to_their_place(partial, other):
    half = lax.axis_size("ctx") // 2
    pairs = []
    for side in range(2):
        for slab in range(half):
            for own in range(2):
                source = (side * half + slab) * 2 + own
                target = ((own ^ other) * half + slab) * 2 + side
                pairs.append((source, target))
    return lax.ppermute(partial, ("ctx", "tp"), pairs)


def project_whole(gated, out_weight):
    sources, _, slab_rows, lanes = gated.shape
    rows = gated.reshape(sources, slab_rows, lanes).transpose(1, 0, 2)
    partials = jnp.dot(
        rows.reshape(slab_rows, sources * lanes),
        lax.all_gather(out_weight, "ctx", axis=1, tiled=True),
        preferred_element_type=jnp.float32,
    )
    return lax.psum_scatter(partials, "tp", scatter_dimension=1, tiled=True).astype(jnp.bfloat16)


def body(qkv_in, short_taps, long_filter, skip_gain, out_weight):
    channel_count = qkv_in.shape[2]
    peers = lax.axis_size("ctx")
    lanes = channel_count // peers
    copies = 2 if lax.axis_size("tp") == 2 and peers == 16 else 1

    packed = pack(qkv_in.transpose(1, 0, 2), short_taps, long_filter, peers)
    arrived = lax.all_to_all(packed, "ctx", split_axis=0, concat_axis=0, tiled=True)
    if copies == 2:
        pieces = weights_from_chips(out_weight, packed, arrived)

    taps = own_columns(short_taps.reshape(-1, channel_count), lanes)
    skip = own_columns(skip_gain[None, :], lanes)
    gated = gated_conv(arrived, taps, skip, qkv_in.shape[0], copies)
    if copies == 2:
        gated, pieces = lax.optimization_barrier((gated, pieces))
        weights = weights_between_cores(pieces)
    by_target = gated.reshape(peers, copies, *gated.shape[3:])
    landed = lax.all_to_all(by_target, "ctx", split_axis=0, concat_axis=0, tiled=True)
    if copies == 2:
        return project_on_halves(landed, weights)
    return project_whole(landed, out_weight)


def solution(mesh):
    return jax.shard_map(
        body,
        mesh=mesh,
        in_specs=(
            P("ctx", None, "tp"),
            P(None, None, "tp"),
            P("ctx", "tp"),
            P("tp"),
            P("tp", "ctx"),
        ),
        out_specs=P("ctx", "tp"),
        check_vma=False,
    )
```

```python
import functools
import itertools

import jax
import jax.numpy as jnp
import numpy as np
from jax import lax
from jax.experimental import pallas as pl
from jax.experimental.pallas import tpu as pltpu
from jax.sharding import PartitionSpec as P

BLOCK = 256
ROWS_AT_ONCE = 8
EDGE_ROWS = 16


def split_bf16(matrix):
    high = matrix.astype(jnp.bfloat16)
    low = (matrix - high.astype(np.float64)).astype(jnp.bfloat16)
    return high, low


@functools.cache
def transform_tables(block):
    freq = np.arange(block)[:, None] + 0.5
    radians = np.pi * freq * np.arange(block)[None, :] / block
    table = np.concatenate([np.cos(radians), -np.sin(radians)], axis=0)
    high, low = split_bf16(table)
    back_high, back_low = split_bf16(table.T / block)
    forward = np.concatenate([high, low], axis=1)
    backward = np.concatenate([back_high, back_low, back_high], axis=1)
    return forward, backward


def blocks_together(lanes, count):
    return 2 if lanes % 128 == 0 and count % 2 == 0 else 1


def forward_into(table_ref, read, count, spectra):
    together = blocks_together(read(0).shape[1], count)
    for first in range(0, count, together):
        columns = [read(first + i) for i in range(together)]
        wide = jnp.concatenate(columns, axis=1) if together > 1 else columns[0]
        spectrum = jnp.dot(
            table_ref[...],
            jnp.concatenate([wide, wide], axis=0),
            preferred_element_type=jnp.float32,
        )
        lanes = columns[0].shape[1]
        for i in range(together):
            spectra[first + i] = spectrum[:, i * lanes : (i + 1) * lanes]


def conv_kernel(
    table_ref,
    back_ref,
    arrived_ref,
    taps_ref,
    skip_ref,
    out_ref,
    spectra,
    filter_ref,
    products,
    padded,
    mixed,
    edges,
):
    block = table_ref.shape[1] // 2
    slabs, _, lanes = arrived_ref.shape
    tokens = mixed.shape[0]
    slab_rows = tokens // slabs
    count = tokens // block
    per_block = block // slab_rows

    def reader(kind):
        begin = kind * slab_rows

        def read(index):
            part = arrived_ref[
                index * per_block : (index + 1) * per_block, begin : begin + slab_rows
            ]
            return part.reshape(block, lanes)

        return read

    for index in range(count):
        mixed[index * block : (index + 1) * block] = reader(2)(index).astype(jnp.float32)
    complete_mixed(arrived_ref, taps_ref, mixed, edges)

    def read_mixed(index):
        return mixed[index * block : (index + 1) * block].astype(jnp.bfloat16)

    forward_into(table_ref, read_mixed, count, spectra)
    forward_into(table_ref, reader(0), count, filter_ref)

    parity = lax.broadcasted_iota(jnp.int32, (block, lanes), 0) % 2
    sign = (1 - 2 * parity).astype(jnp.float32)
    for index in range(count - 1, 0, -1):
        before_real = filter_ref[index - 1, :block]
        before_imag = filter_ref[index - 1, block:]
        filter_ref[index, :block] = filter_ref[index, :block] - sign * before_imag
        filter_ref[index, block:] = filter_ref[index, block:] + sign * before_real

    margin = padded.shape[0] - tokens
    padded[:margin] = jnp.zeros((margin, lanes), jnp.float32)
    for index in range(count):
        at = margin + index * block
        padded[at : at + block] = reader(1)(index).astype(jnp.float32)

    def rows_step(step, carry):
        at = pl.multiple_of(step * ROWS_AT_ONCE, ROWS_AT_ONCE)
        real_rows = pl.ds(at, ROWS_AT_ONCE)
        imag_rows = pl.ds(pl.multiple_of(block + at, ROWS_AT_ONCE), ROWS_AT_ONCE)
        signal_real = [spectra[i, real_rows] for i in range(count)]
        signal_imag = [spectra[i, imag_rows] for i in range(count)]
        filter_real = [filter_ref[i, real_rows] for i in range(count)]
        filter_imag = [filter_ref[i, imag_rows] for i in range(count)]
        for target in range(count):
            real = imag = None
            for source in range(target + 1):
                a, b = signal_real[source], signal_imag[source]
                c, d = filter_real[target - source], filter_imag[target - source]
                term_real = a * c - b * d
                term_imag = a * d + b * c
                real = term_real if real is None else real + term_real
                imag = term_imag if imag is None else imag + term_imag
            products[target, real_rows] = real
            products[target, imag_rows] = imag
        return carry

    def long_step(target, carry):
        def add(source, totals):
            a, b = spectra[source, :block], spectra[source, block:]
            c, d = filter_ref[target - source, :block], filter_ref[target - source, block:]
            return totals[0] + (a * c - b * d), totals[1] + (a * d + b * c)

        zero = jnp.zeros((block, lanes), jnp.float32)
        real, imag = lax.fori_loop(0, target + 1, add, (zero, zero))
        products[target, :block] = real
        products[target, block:] = imag
        return carry

    if count <= 8:
        lax.fori_loop(0, block // ROWS_AT_ONCE, rows_step, 0)
    else:
        lax.fori_loop(0, count, long_step, 0)

    together = blocks_together(lanes, count)
    for first in range(0, count, together):
        parts = [products[first + i] for i in range(together)]
        wide = jnp.concatenate(parts, axis=1) if together > 1 else parts[0]
        high = wide.astype(jnp.bfloat16)
        low = (wide - high.astype(jnp.float32)).astype(jnp.bfloat16)
        rows = jnp.dot(
            back_ref[...],
            jnp.concatenate([high, high, low], axis=0),
            preferred_element_type=jnp.float32,
        )
        for i in range(together):
            at = (first + i) * block
            convolved = rows[:, i * lanes : (i + 1) * lanes]
            begin = margin + at
            queries = taps_ref[0:1, :] * padded[begin : begin + block]
            for tap in range(1, taps_ref.shape[0] // 3):
                shifted = padded[begin - tap : begin - tap + block]
                queries = queries + taps_ref[tap : tap + 1, :] * shifted
            gated = queries * (convolved + skip_ref[...] * mixed[at : at + block])
            store_gated(out_ref, at, gated.astype(out_ref.dtype))


def complete_mixed(arrived_ref, taps_ref, mixed, edges):
    slabs = arrived_ref.shape[0]
    slab_rows = mixed.shape[0] // slabs
    taps = taps_ref.shape[0] // 3
    reach = taps - 1
    edges[:EDGE_ROWS] = jnp.zeros((EDGE_ROWS, edges.shape[1]), jnp.float32)
    for slab in range(slabs):
        at = (slab + 1) * EDGE_ROWS
        edges[at : at + EDGE_ROWS] = arrived_ref[slab, 3 * slab_rows :].astype(jnp.float32)

    def raw(kind, row):
        if row >= 0:
            return edges[pl.ds(EDGE_ROWS + kind * reach + row, slabs, stride=EDGE_ROWS), :]
        return edges[pl.ds((kind + 3) * reach + row, slabs, stride=EDGE_ROWS), :]

    for row in range(reach):
        product = None
        for kind in range(2):
            base = (kind + 1) * taps
            feature = taps_ref[base : base + 1, :] * raw(kind, row)
            for tap in range(1, taps):
                feature = feature + taps_ref[base + tap : base + tap + 1, :] * raw(kind, row - tap)
            product = feature if product is None else product * feature
        rounded = product.astype(jnp.bfloat16).astype(jnp.float32)
        mixed[pl.ds(row, slabs, stride=slab_rows), :] = rounded


def store_gated(out_ref, at, gated):
    copies, per_half, _, slab_rows, _ = out_ref.shape
    for begin in range(0, gated.shape[0], slab_rows):
        slab = (at + begin) // slab_rows
        for copy in range(copies):
            out_ref[copy, slab % per_half, slab // per_half] = gated[begin : begin + slab_rows]


def project_kernel(parts, own_ref, gated_ref, *refs):
    weight_refs, (near_ref, far_ref, rows) = iter(refs[:-3]), refs[-3:]
    sources, count, lanes = gated_ref.shape
    for source in range(sources):
        rows[:, source * lanes : (source + 1) * lanes] = gated_ref[source]
    swap = own_ref[0] == 1
    columns = near_ref.shape[1] // len(parts)
    for block, part_count in enumerate(parts):
        sums, begin = None, 0
        for weight_ref in itertools.islice(weight_refs, part_count):
            end = begin + weight_ref.shape[0]
            added = jnp.dot(rows[:, begin:end], weight_ref[...], preferred_element_type=jnp.float32)
            sums, begin = added if sums is None else sums + added, end
        first = sums[: count // 2].astype(near_ref.dtype)
        second = sums[count // 2 :].astype(near_ref.dtype)
        target = slice(block * columns, (block + 1) * columns)
        near_ref[:, target] = jnp.where(swap, second, first)
        far_ref[:, target] = jnp.where(swap, first, second)


def finish_kernel(first_offsets, place_ref, *refs):
    *pair_refs, out_ref = refs
    offset = 0
    for at, count in enumerate(first_offsets):
        near_ref, far_ref = pair_refs[2 * at : 2 * at + 2]
        columns = near_ref.shape[1] // count
        for block in range(count):
            source = slice(block * columns, (block + 1) * columns)
            total = near_ref[:, source].astype(jnp.float32) + far_ref[:, source].astype(jnp.float32)
            begin = (place_ref[0] ^ offset) * columns
            out_ref[:, pl.ds(pl.multiple_of(begin, columns), columns)] = total.astype(out_ref.dtype)
            offset += 1


def pack_kernel(qkv_ref, taps_ref, filter_ref, out_ref, padded, edges):
    targets, _, lanes = out_ref.shape
    rows = filter_ref.shape[0]
    reach = taps_ref.shape[1] - 1
    margin = padded.shape[1] - rows
    edges[4 * reach :] = jnp.zeros((edges.shape[0] - 4 * reach, edges.shape[1]), jnp.float32)
    raw = [qkv_ref[kind].astype(jnp.float32) for kind in (1, 2)]
    for kind in range(2):
        padded[kind, :margin] = jnp.zeros((margin, padded.shape[2]), jnp.float32)
        padded[kind, margin:] = raw[kind]
    mixed_in = None
    for kind in range(2):
        feature = taps_ref[kind + 1, 0:1] * raw[kind]
        for tap in range(1, reach + 1):
            shifted = padded[kind, margin - tap : margin - tap + rows]
            feature = feature + taps_ref[kind + 1, tap : tap + 1] * shifted
        mixed_in = feature if mixed_in is None else mixed_in * feature
        edges[kind * reach : (kind + 1) * reach] = padded[kind, margin : margin + reach]
        edges[(kind + 2) * reach : (kind + 3) * reach] = padded[kind, margin + rows - reach :]
    for target in range(targets):
        at = slice(target * lanes, (target + 1) * lanes)
        out_ref[target, :rows] = filter_ref[:, at].astype(out_ref.dtype)
        out_ref[target, rows : 2 * rows] = qkv_ref[0, :, at]
        out_ref[target, 2 * rows : 3 * rows] = mixed_in[:, at].astype(out_ref.dtype)
        out_ref[target, 3 * rows :] = edges[:, at].astype(out_ref.dtype)


def pack(by_kind, short_taps, long_filter, peers):
    kinds, rows, channels = by_kind.shape
    reach = short_taps.shape[1] - 1
    lanes = channels // peers
    total = 3 * rows + EDGE_ROWS
    if lanes % 128:
        features = []
        for kind in (1, 2):
            extended = jnp.pad(by_kind[kind].astype(jnp.float32), ((reach, 0), (0, 0)))
            feature = short_taps[kind, 0] * extended[reach:]
            for tap in range(1, reach + 1):
                feature = feature + short_taps[kind, tap] * extended[reach - tap : reach - tap + rows]
            features.append(feature)
        mixed_in = (features[0] * features[1]).astype(jnp.bfloat16)
        first = by_kind[1:, :reach].reshape(2 * reach, channels)
        last = by_kind[1:, rows - reach :].reshape(2 * reach, channels)
        spare = jnp.zeros((EDGE_ROWS - 4 * reach, channels), jnp.bfloat16)
        parts = [long_filter.astype(jnp.bfloat16), by_kind[0], mixed_in, first, last, spare]
        return jnp.concatenate(parts).reshape(total, peers, lanes).transpose(1, 0, 2)
    steps = 2 if peers % 2 == 0 else 1
    width = channels // steps
    return pl.pallas_call(
        pack_kernel,
        out_shape=jax.ShapeDtypeStruct((peers, total, lanes), jnp.bfloat16),
        grid=(steps,),
        in_specs=[
            pl.BlockSpec((kinds, rows, width), lambda i: (0, 0, i)),
            pl.BlockSpec((kinds, reach + 1, width), lambda i: (0, 0, i)),
            pl.BlockSpec((rows, width), lambda i: (0, i)),
        ],
        out_specs=pl.BlockSpec((peers // steps, total, lanes), lambda i: (i, 0, 0)),
        scratch_shapes=[
            pltpu.VMEM((2, rows + 8, width), jnp.float32),
            pltpu.VMEM((EDGE_ROWS, width), jnp.float32),
        ],
        compiler_params=pltpu.CompilerParams(vmem_limit_bytes=60 * 2**20),
        cost_estimate=pl.CostEstimate(
            flops=16 * rows * channels, bytes_accessed=16 * rows * channels, transcendentals=0
        ),
        name="pack",
    )(by_kind, short_taps, long_filter)


def gated_conv(arrived, taps, skip, slab_rows, copies):
    slabs, _, lanes = arrived.shape
    tokens = slabs * slab_rows
    forward, backward = transform_tables(BLOCK)
    spectra = pltpu.VMEM((tokens // BLOCK, 2 * BLOCK, lanes), jnp.float32)
    return pl.pallas_call(
        conv_kernel,
        out_shape=jax.ShapeDtypeStruct(
            (copies, slabs // copies, copies, slab_rows, lanes), jnp.bfloat16
        ),
        scratch_shapes=[spectra] * 3
        + [
            pltpu.VMEM((tokens + 8, lanes), jnp.float32),
            pltpu.VMEM((tokens, lanes), jnp.float32),
            pltpu.VMEM(((slabs + 1) * EDGE_ROWS, lanes), jnp.float32),
        ],
        compiler_params=pltpu.CompilerParams(
            vmem_limit_bytes=(48 if tokens > 2048 else 20) * 2**20
        ),
        cost_estimate=pl.CostEstimate(
            flops=28 * BLOCK * tokens * lanes, bytes_accessed=20 * tokens * lanes, transcendentals=0
        ),
        name="gated_conv",
    )(jnp.asarray(forward), jnp.asarray(backward), arrived, taps, skip)


def project(own, gated, weights):
    sources, count, lanes = gated.shape
    depth, columns = sources * lanes, weights[0][0].shape[1]
    half = jax.ShapeDtypeStruct((count // 2, len(weights) * columns), jnp.bfloat16)
    whole = pl.BlockSpec(memory_space=pltpu.VMEM)
    flat = [part for parts in weights for part in parts]
    return pl.pallas_call(
        functools.partial(project_kernel, [len(parts) for parts in weights]),
        out_shape=(half, half),
        in_specs=[pl.BlockSpec(memory_space=pltpu.SMEM)] + [whole] * (1 + len(flat)),
        out_specs=(whole, whole),
        scratch_shapes=[pltpu.VMEM((count, depth), jnp.bfloat16)],
        compiler_params=pltpu.CompilerParams(vmem_limit_bytes=20 * 2**20),
        cost_estimate=pl.CostEstimate(
            flops=2 * count * depth * len(weights) * columns,
            bytes_accessed=2 * depth * len(weights) * columns + 4 * count * depth,
            transcendentals=0,
        ),
        name="project",
    )(own, gated, *flat)


def finish(place, pairs, blocks):
    rows = pairs[0][0].shape[0]
    columns = sum(near.shape[1] for near, _ in pairs)
    whole = pl.BlockSpec(memory_space=pltpu.VMEM)
    return pl.pallas_call(
        functools.partial(finish_kernel, blocks),
        out_shape=jax.ShapeDtypeStruct((rows, columns), jnp.bfloat16),
        in_specs=[pl.BlockSpec(memory_space=pltpu.SMEM)] + [whole] * (2 * len(pairs)),
        out_specs=whole,
        compiler_params=pltpu.CompilerParams(vmem_limit_bytes=20 * 2**20),
        cost_estimate=pl.CostEstimate(
            flops=rows * columns, bytes_accessed=6 * rows * columns, transcendentals=0
        ),
        name="finish",
    )(place, *[partial for pair in pairs for partial in pair])


def own_columns(array, lanes):
    return lax.dynamic_slice_in_dim(array, lax.axis_index("ctx") * lanes, lanes, axis=1)


def from_partner(value, offset):
    pairs = [(i, i ^ offset) for i in range(lax.axis_size("ctx"))]
    return lax.ppermute(value, "ctx", pairs)


def after(values, *others):
    return lax.optimization_barrier((values, others))[0]


def weights_from_chips(out_weight, packed, arrived):
    cut = out_weight.shape[0] // 16 * 7
    own = after(out_weight, packed)
    x_piece = from_partner(own, 2)
    z_first, rest = after((from_partner(own[:cut], 4), own[cut:]), arrived)
    return {
        0: [out_weight],
        2: [x_piece],
        4: [z_first, from_partner(rest, 4)],
        6: [from_partner(z_first, 2)],
    }


def weights_between_cores(pieces):
    pieces = {**pieces, 6: pieces[6] + [from_partner(pieces[4][1], 2)]}
    for at in (1, 3, 5):
        pieces[at] = [from_partner(part, 1) for part in pieces[at ^ 1]]
    pieces[7] = [from_partner(pieces[6][0], 1)]
    return [pieces[at] for at in range(8)]


def project_on_halves(gated, weights):
    half = lax.axis_size("ctx") // 2
    sources, halves, slab_rows, lanes = gated.shape
    rows = gated.reshape(sources, halves * slab_rows, lanes)
    own = lax.axis_index("tp").astype(jnp.int32)[None]
    place = (lax.axis_index("ctx") % half).astype(jnp.int32)[None]
    split = len(weights) // 2
    first = project(own, rows, weights[:split])
    last_part, _ = lax.optimization_barrier((weights[6][-1], first[0]))
    weights[7] = weights[7] + [from_partner(last_part, 1)]
    second = project(own, rows, weights[split:])
    arrived = [
        [to_their_place(partial, other) for other, partial in enumerate(partials)]
        for partials in (first, second)
    ]
    return finish(place, arrived, [split, len(weights) - split])


def to_their_place(partial, other):
    half = lax.axis_size("ctx") // 2
    pairs = []
    for side in range(2):
        for slab in range(half):
            for own in range(2):
                source = (side * half + slab) * 2 + own
                target = ((own ^ other) * half + slab) * 2 + side
                pairs.append((source, target))
    return lax.ppermute(partial, ("ctx", "tp"), pairs)


def project_whole(gated, out_weight):
    sources, _, slab_rows, lanes = gated.shape
    rows = gated.reshape(sources, slab_rows, lanes).transpose(1, 0, 2)
    partials = jnp.dot(
        rows.reshape(slab_rows, sources * lanes),
        lax.all_gather(out_weight, "ctx", axis=1, tiled=True),
        preferred_element_type=jnp.float32,
    )
    return lax.psum_scatter(partials, "tp", scatter_dimension=1, tiled=True).astype(jnp.bfloat16)


def body(qkv_in, short_taps, long_filter, skip_gain, out_weight):
    channel_count = qkv_in.shape[2]
    peers = lax.axis_size("ctx")
    lanes = channel_count // peers
    copies = 2 if lax.axis_size("tp") == 2 and peers == 16 else 1

    packed = pack(qkv_in.transpose(1, 0, 2), short_taps, long_filter, peers)
    arrived = lax.all_to_all(packed, "ctx", split_axis=0, concat_axis=0, tiled=True)
    if copies == 2:
        pieces = weights_from_chips(out_weight, packed, arrived)

    taps = own_columns(short_taps.reshape(-1, channel_count), lanes)
    skip = own_columns(skip_gain[None, :], lanes)
    gated = gated_conv(arrived, taps, skip, qkv_in.shape[0], copies)
    if copies == 2:
        gated, pieces = lax.optimization_barrier((gated, pieces))
        weights = weights_between_cores(pieces)
    by_target = gated.reshape(peers, copies, *gated.shape[3:])
    landed = lax.all_to_all(by_target, "ctx", split_axis=0, concat_axis=0, tiled=True)
    if copies == 2:
        return project_on_halves(landed, weights)
    return project_whole(landed, out_weight)


def solution(mesh):
    return jax.shard_map(
        body,
        mesh=mesh,
        in_specs=(
            P("ctx", None, "tp"),
            P(None, None, "tp"),
            P("ctx", "tp"),
            P("tp"),
            P("tp", "ctx"),
        ),
        out_specs=P("ctx", "tp"),
        check_vma=False,
    )
```
